256 devices in a mesh: section: 4 (over y_lo, core), expert: 32 (over z, x), dp: 2 (over y_hi).
Axes of the slice: x: 4, y: 4 (y_hi: 2, y_lo: 2; y = y_hi * 2 + y_lo), z: 8, core: 2. Of those that a mesh axis runs over, the one named last changes fastest.
Arguments:
- fwd_in: bfloat16 [4, 8192, 2048], P('section', ('expert', 'dp')), may hold values from -6 to 6
- saved_in: bfloat16 [4, 8192, 2048], P('section', ('expert', 'dp')), may hold values from -6 to 6
- out_grad: bfloat16 [4, 8192, 2048], P('section', ('expert', 'dp')), may hold values from -6 to 6
- gain: bfloat16 [4, 2048], P('section'), may hold values from 0.25 to 1.75
- router: bfloat16 [4, 2048, 32], P('section'), may hold values from -0.25 to 0.25
- w_gate: bfloat16 [4, 32, 2048, 704], P('section', 'expert', None, 'dp'), may hold values from -0.125 to 0.125
- w_up: bfloat16 [4, 32, 2048, 704], P('section', 'expert', None, 'dp'), may hold values from -0.125 to 0.125
- w_down: bfloat16 [4, 32, 704, 2048], P('section', 'expert', 'dp'), may hold values from -0.21875 to 0.21875
- routes_fwd: int32 [4, 8192, 2], P('section', ('expert', 'dp')), may hold values from 0 to 31, all different within a row; in each aligned block of 128 rows (0 to 127, 128 to 255, ..., all dimensions but the last counted through in order) at most 12 rows name the same one
- routes_bwd: int32 [4, 8192, 2], P('section', ('expert', 'dp')), may hold values from 0 to 31, all different within a row; in each aligned block of 128 rows (0 to 127, 128 to 255, ..., all dimensions but the last counted through in order) at most 12 rows name the same one
Outputs:
- sent_fwd: bfloat16 [4, 8192, 2048], P('section', ('expert', 'dp'))
- sent_bwd: bfloat16 [4, 8192, 2048], P('section', ('expert', 'dp'))
- grad_gate: bfloat16 [4, 32, 2048, 704], P('section', 'expert', None, 'dp')
- grad_up: bfloat16 [4, 32, 2048, 704], P('section', 'expert', None, 'dp')
- grad_down: bfloat16 [4, 32, 704, 2048], P('section', 'expert', 'dp')
- grad_router: float32 [4, 2048, 32], P('section')
- grad_gain: float32 [4, 2048], P('section')
The draws below stay inside these ranges and needn't reach their ends.
Inputs may be any that keep to these rules, and one draw needn't show every extreme that they name: `routes_fwd`: each token names 2 different experts. In each aligned block of 128 tokens (the tokens of one device) no expert is named by more than 12 tokens, and in every draw some block has an expert named by exactly 12. `routes_bwd`: as for routes_fwd.
All inputs are finite; a program needn't handle non-finite values.
Results may differ from the reference program's by a relative error of at most 0.019.
Values may be sent and summed in bfloat16 or wider, within the bound.
A program may use at most 128 MiB of HBM per device.

```python
import math
import jax
import jax.numpy as jnp
import numpy as np
from jax import lax

D = 2048
FFE = 704
TOP = 2
TOK_DEV = 128
EXPERTS = 32
TOKENS = 8192
CAP = 12
N_SECTION = 4


def level_of(stream_key, extent, pieces, low, high):
    level = 1.0
    for axis_at, blocks in pieces:
        draws = jax.random.uniform(jax.random.fold_in(jax.random.fold_in(stream_key, 6), axis_at), (blocks,), jnp.float32, low / len(pieces), high / len(pieces))
        level = level * jnp.repeat(jnp.exp(draws), extent[axis_at] // blocks).reshape((-1,) + (1,) * (len(extent) - 1 - axis_at))
    return level


def routed_block(key, own, number, rows, number_of, top, most, skew):
    sequence = jax.random.permutation(key, number_of)
    crowded, ordinary = portions_of(number_of, rows * top, most, skew, True), portions_of(number_of, rows * top, most, skew, False)
    places = jnp.arange(number_of)

    def named(sizes, turn):
        used = int((sizes > 0).sum())
        fixed = max(1, used // 4)
        moved = fixed + (places - fixed + turn * (used - fixed)) % max(1, number_of - fixed)
        return jnp.zeros((number_of,), jnp.int32).at[sequence[jnp.where(places < fixed, places, moved)]].set(jnp.asarray(sizes, jnp.int32))

    sizes = jnp.where(number % 4 == 0, named(crowded, number // 4), named(ordinary, number - number // 4 - 1))
    mixed = jax.random.permutation(jax.random.fold_in(own, 3), number_of)
    donor, taker = mixed[0:number_of // 2 * 2:2], mixed[1:number_of // 2 * 2:2]
    slack = jnp.minimum(sizes[donor] - 1, most - sizes[taker]) // 2
    slack = jnp.where((donor == sequence[0]) | (taker == sequence[0]) | (sizes[taker] == 0), 0, jnp.maximum(slack, 0))
    moved = jax.random.randint(jax.random.fold_in(own, 4), (number_of // 2,), 0, 1 << 20) % (slack + 1)
    sizes = sizes.at[donor].add(-moved).at[taker].add(moved)
    items = jnp.searchsorted(jnp.cumsum(sizes), jnp.arange(rows * top), side="right").astype(jnp.int32)
    grid = items.reshape(top, rows).T
    grid = grid[jax.random.permutation(jax.random.fold_in(own, 1), rows)]
    turn = jax.random.randint(jax.random.fold_in(own, 2), (rows, 1), 0, top)
    return jnp.take_along_axis(grid, (jnp.arange(top)[None, :] + turn) % top, axis=1)


def portions_of(number_of, total, most, lean, full):
    weights = [(1 << 20) // math.isqrt(rank ** lean) + 1 for rank in range(1, number_of + 1)]
    largest = most if full else min(most, max(-(-total // number_of), total * weights[0] // sum(weights)))
    least = 1 if total - largest >= number_of - 1 else 0
    given, surplus = [largest] + [least] * (number_of - 1), total - largest - least * (number_of - 1)
    while surplus > 0:
        movable = [i for i in range(1, number_of) if given[i] < largest] or [i for i in range(1, number_of) if given[i] < most]
        pool, remaining = sum([weights[i] for i in movable]), surplus
        for i in movable:
            addition = min(most - given[i], max(1, remaining * weights[i] // pool), surplus)
            given[i] = given[i] + addition
            surplus = surplus - addition
    return np.array(given)


def normal_values(stream_key, shape, scale, limit, cuts=(), kind=jnp.bfloat16):
    loudness = level_of(stream_key, shape, cuts, -0.22, 0.18) if cuts else 1.0
    values = jax.random.normal(stream_key, shape, jnp.float32) * scale * loudness
    return jnp.minimum(jnp.maximum(values, -limit), limit).astype(kind)


def setup_inputs(seed: int = 0) -> dict:
    seeds = jax.random.split(jax.random.key(seed), 11)
    fwd_in = normal_values(seeds[0], (N_SECTION, TOKENS, D), 1.0, 6.0, ((0, 4), (1, 64)))
    saved_in = normal_values(seeds[1], (N_SECTION, TOKENS, D), 1.0, 6.0, ((0, 4), (1, 64)))
    out_grad = normal_values(seeds[2], (N_SECTION, TOKENS, D), 1.0, 6.0, ((0, 4), (1, 64)))
    gain = jnp.clip(1.0 + 0.15 * jax.random.normal(seeds[3], (N_SECTION, D), jnp.float32), 0.25, 1.75).astype(jnp.bfloat16)
    router = normal_values(seeds[4], (N_SECTION, D, EXPERTS), (D // 4) ** -0.5, 0.25, ((0, 4),))
    w_gate = normal_values(seeds[5], (N_SECTION, EXPERTS, D, FFE), D ** -0.5, 0.125, ((0, 4), (1, 32), (3, 2)))
    w_up = normal_values(seeds[6], (N_SECTION, EXPERTS, D, FFE), D ** -0.5, 0.125, ((0, 4), (1, 32), (3, 2)))
    w_down = normal_values(seeds[7], (N_SECTION, EXPERTS, FFE, D), FFE ** -0.5, 0.21875, ((0, 4), (1, 32), (2, 2)))
    routes_fwd_keys = jax.random.split(jax.random.fold_in(seeds[8], 1), N_SECTION * TOKENS // TOK_DEV)
    routes_fwd_turns = jax.random.permutation(jax.random.fold_in(seeds[8], 3), N_SECTION * TOKENS // TOK_DEV)
    routes_fwd = jax.vmap(lambda own, number: routed_block(jax.random.fold_in(seeds[8], 2), own, number, TOK_DEV, EXPERTS, TOP, CAP, 2))(routes_fwd_keys, routes_fwd_turns).reshape((N_SECTION, TOKENS, TOP))
    routes_bwd_keys = jax.random.split(jax.random.fold_in(seeds[9], 1), N_SECTION * TOKENS // TOK_DEV)
    routes_bwd_turns = jax.random.permutation(jax.random.fold_in(seeds[9], 3), N_SECTION * TOKENS // TOK_DEV)
    routes_bwd = jax.vmap(lambda own, number: routed_block(jax.random.fold_in(seeds[9], 2), own, number, TOK_DEV, EXPERTS, TOP, CAP, 2))(routes_bwd_keys, routes_bwd_turns).reshape((N_SECTION, TOKENS, TOP))
    return dict(fwd_in=fwd_in, saved_in=saved_in, out_grad=out_grad, gain=gain, router=router, w_gate=w_gate, w_up=w_up, w_down=w_down, routes_fwd=routes_fwd, routes_bwd=routes_bwd)


EPS = 1e-06

def norm_rows(inputs, gain_row):
    as_float = inputs.astype(jnp.float32)
    inverse = lax.rsqrt(lax.optimization_barrier(jnp.mean(as_float * as_float, axis=-1, keepdims=True)) + EPS)
    normed = (as_float * inverse * gain_row.astype(jnp.float32)).astype(jnp.bfloat16)
    return (as_float, inverse, normed)

def router_gates(normed, router_mat, routes):
    logits = jnp.dot(normed, router_mat, preferred_element_type=jnp.float32)
    experts = router_mat.shape[1]
    selector = (routes[:, :, None] == jnp.arange(experts, dtype=jnp.int32)[None, None, :]).astype(jnp.float32)
    chosen = lax.optimization_barrier(jnp.sum(selector * logits[:, None, :], axis=-1))
    return (jax.nn.sigmoid(chosen), selector)

def route_slots(routes, experts, capacity):
    count = routes.shape[0] * routes.shape[1]
    flat = routes.reshape(count).astype(jnp.int32)
    onehot = (flat[:, None] == jnp.arange(experts, dtype=jnp.int32)[None, :]).astype(jnp.int32)
    before = jnp.cumsum(onehot, axis=0) - onehot
    slots = lax.optimization_barrier(jnp.sum(before * onehot, axis=1))
    return (flat * capacity + slots).astype(jnp.int32)

def expert_result(rows_in, gate_weight, up_weight, down_weight):
    pre_gate = jnp.dot(rows_in, gate_weight, preferred_element_type=jnp.float32)
    pre_up = jnp.dot(rows_in, up_weight, preferred_element_type=jnp.float32)
    hidden = (pre_gate * jax.nn.sigmoid(pre_gate) * pre_up).astype(jnp.bfloat16)
    return jnp.dot(hidden, down_weight, preferred_element_type=jnp.float32)

def backward_core(rows_in, grad_out, gate_weight, up_weight, down_weight):
    contract_rows = (((0,), (0,)), ((), ()))
    contract_cols = (((1,), (1,)), ((), ()))
    pre_gate = jnp.dot(rows_in, gate_weight, preferred_element_type=jnp.float32)
    pre_up = jnp.dot(rows_in, up_weight, preferred_element_type=jnp.float32)
    sigm_gate = jax.nn.sigmoid(pre_gate)
    swish = pre_gate * sigm_gate
    hidden = (swish * pre_up).astype(jnp.bfloat16)
    result = jnp.dot(hidden, down_weight, preferred_element_type=jnp.float32)
    grad_hidden = lax.dot_general(grad_out, down_weight, contract_cols, preferred_element_type=jnp.float32)
    grad_pre_up = (grad_hidden * swish).astype(jnp.bfloat16)
    grad_pre_gate = (grad_hidden * pre_up * sigm_gate * (1.0 + pre_gate * (1.0 - sigm_gate))).astype(jnp.bfloat16)
    grad_down_w = lax.dot_general(hidden, grad_out, contract_rows, preferred_element_type=jnp.float32)
    grad_gate_w = lax.dot_general(rows_in, grad_pre_gate, contract_rows, preferred_element_type=jnp.float32)
    grad_up_w = lax.dot_general(rows_in, grad_pre_up, contract_rows, preferred_element_type=jnp.float32)
    grad_rows = lax.dot_general(grad_pre_gate, gate_weight, contract_cols, preferred_element_type=jnp.float32)
    grad_rows = grad_rows + lax.dot_general(grad_pre_up, up_weight, contract_cols, preferred_element_type=jnp.float32)
    return (result, grad_rows, grad_gate_w, grad_up_w, grad_down_w)

def expert_backward(rows_in, cot_rows, gate_rows, gate_weight, up_weight, down_weight):
    grad_out = (gate_rows[:, None] * cot_rows.astype(jnp.float32)).astype(jnp.bfloat16)
    result, grad_rows, grad_gate_w, grad_up_w, grad_down_w = backward_core(rows_in, grad_out, gate_weight, up_weight, down_weight)
    result = result.astype(jnp.bfloat16)
    gate_grad = lax.optimization_barrier(jnp.sum(result.astype(jnp.float32) * cot_rows.astype(jnp.float32), axis=1))
    return (gate_grad, grad_rows.astype(jnp.bfloat16), grad_gate_w.astype(jnp.bfloat16), grad_up_w.astype(jnp.bfloat16), grad_down_w.astype(jnp.bfloat16))

def pack_rows(targets, values, slots):

    def place_one(target, value):
        return jnp.zeros((slots,) + value.shape[1:], value.dtype).at[target].set(value)
    return jax.vmap(place_one)(targets, values)

def by_expert(packed):
    blocks = packed.shape[0]
    others = packed.shape[2:]
    shaped = packed.reshape((blocks, EXPERTS, CAP) + others)
    return jnp.moveaxis(shaped, 0, 1).reshape((EXPERTS, blocks * CAP) + others)

def by_block(expert_rows, blocks):
    others = expert_rows.shape[2:]
    shaped = expert_rows.reshape((EXPERTS, blocks, CAP) + others)
    return jnp.moveaxis(shaped, 1, 0).reshape((blocks, EXPERTS * CAP) + others)

def pick_rows(returned, targets):
    return jax.vmap(lambda lookup, target: lookup[target])(returned, targets)

def block_targets(routes, blocks):
    return jax.vmap(lambda chosen: route_slots(chosen, EXPERTS, CAP))(routes.reshape(blocks, TOK_DEV, TOP))

def forward_section(inputs, gain_row, router_mat, gate_weight, up_weight, down_weight, routes):
    blocks = TOKENS // TOK_DEV
    as_float, inverse, normed = norm_rows(inputs, gain_row)
    gate_vals, selector = router_gates(normed, router_mat, routes)
    targets = block_targets(routes, blocks)
    repeated = jnp.repeat(normed.reshape(blocks, TOK_DEV, D), TOP, axis=1)
    expert_rows = by_expert(pack_rows(targets, repeated, EXPERTS * CAP))
    results = lax.map(lambda operands: expert_result(*operands).astype(jnp.bfloat16), (expert_rows, gate_weight, up_weight, down_weight))
    picked = pick_rows(by_block(results, blocks), targets).reshape(TOKENS, TOP, D)
    mixed = as_float + lax.optimization_barrier(jnp.sum(gate_vals[:, :, None] * picked.astype(jnp.float32), axis=1))
    return mixed.astype(jnp.bfloat16)

def backward_section(inputs, cotangent, gain_row, router_mat, gate_weight, up_weight, down_weight, routes):
    blocks = TOKENS // TOK_DEV
    as_float, inverse, normed = norm_rows(inputs, gain_row)
    gate_vals, selector = router_gates(normed, router_mat, routes)
    targets = block_targets(routes, blocks)
    slots = EXPERTS * CAP
    expert_rows = by_expert(pack_rows(targets, jnp.repeat(normed.reshape(blocks, TOK_DEV, D), TOP, axis=1), slots))
    cot_rows = by_expert(pack_rows(targets, jnp.repeat(cotangent.reshape(blocks, TOK_DEV, D), TOP, axis=1), slots))
    gate_rows = by_expert(pack_rows(targets, gate_vals.reshape(blocks, TOK_DEV * TOP), slots))
    gate_grad, grad_rows, grad_gate_w, grad_up_w, grad_down_w = lax.map(lambda operands: expert_backward(*operands), (expert_rows, cot_rows, gate_rows, gate_weight, up_weight, down_weight))
    picked_rows = pick_rows(by_block(grad_rows, blocks), targets).reshape(TOKENS, TOP, D)
    picked_gate = pick_rows(by_block(gate_grad, blocks), targets).reshape(TOKENS, TOP)
    dsel = picked_gate * gate_vals * (1.0 - gate_vals)
    dlogits = lax.optimization_barrier(jnp.sum(selector * dsel[:, :, None], axis=1)).astype(jnp.bfloat16)
    grad_router = lax.dot_general(normed, dlogits, (((0,), (0,)), ((), ())), preferred_element_type=jnp.float32)
    dnormed = lax.optimization_barrier(jnp.sum(picked_rows.astype(jnp.float32), axis=1))
    dnormed = dnormed + lax.dot_general(dlogits, router_mat, (((1,), (1,)), ((), ())), preferred_element_type=jnp.float32)
    scaled = dnormed * gain_row.astype(jnp.float32)
    grad_gain = lax.optimization_barrier(jnp.sum(dnormed * as_float * inverse, axis=0))
    in_grad = cotangent.astype(jnp.float32) + inverse * scaled
    in_grad = in_grad - as_float * inverse ** 3 * lax.optimization_barrier(jnp.mean(scaled * as_float, axis=-1, keepdims=True))
    return (in_grad.astype(jnp.bfloat16), grad_gate_w, grad_up_w, grad_down_w, grad_router, grad_gain)

def reference(fwd_in, saved_in, out_grad, gain, router, w_gate, w_up, w_down, routes_fwd, routes_bwd):
    outputs = []
    backs = []
    for layer_index in range(N_SECTION):
        outputs.append(forward_section(fwd_in[layer_index], gain[layer_index], router[layer_index], w_gate[layer_index], w_up[layer_index], w_down[layer_index], routes_fwd[layer_index]))
        backs.append(backward_section(saved_in[layer_index], out_grad[layer_index], gain[layer_index], router[layer_index], w_gate[layer_index], w_up[layer_index], w_down[layer_index], routes_bwd[layer_index]))
    sent_fwd = jnp.roll(jnp.stack(outputs), 1, axis=0)
    sent_bwd = jnp.roll(jnp.stack([entry[0] for entry in backs]), -1, axis=0)
    grad_gate = jnp.stack([entry[1] for entry in backs])
    grad_up = jnp.stack([entry[2] for entry in backs])
    grad_down = jnp.stack([entry[3] for entry in backs])
    grad_router = jnp.stack([entry[4] for entry in backs])
    grad_gain = jnp.stack([entry[5] for entry in backs])
    return (sent_fwd, sent_bwd, grad_gate, grad_up, grad_down, grad_router, grad_gain)
```

```python
import functools

import jax
import jax.numpy as jnp
from jax import lax
from jax.experimental import pallas as pl
from jax.experimental.pallas import tpu as pltpu
from jax.sharding import PartitionSpec as P

EPS = 1e-06
MESH = pl.DeviceIdType.MESH
EXPERTS = 32
CAP = 12
GROUPS = 3
QUARTS = 4
SLAB = 512
BLOCK = 16
F32 = jnp.float32
BF16 = jnp.bfloat16


def peer_of(me, step):
    return lax.rem(me // 4 + step // 4, 8) * 4 + lax.rem(me + step, 4)


def remote(src, dst, send_sem, recv_sem, device):
    return pltpu.make_async_remote_copy(
        src_ref=src,
        dst_ref=dst,
        send_sem=send_sem,
        recv_sem=recv_sem,
        device_id=device,
        device_id_type=MESH,
    )


def enter(me, other):
    barrier = pltpu.get_barrier_semaphore()

    @pl.loop(1, EXPERTS)
    def _(step):
        pl.semaphore_signal(
            barrier, inc=1, device_id={"expert": peer_of(me, step)}, device_id_type=MESH
        )

    pl.semaphore_signal(barrier, inc=1, device_id={"dp": other}, device_id_type=MESH)
    pl.semaphore_wait(barrier, EXPERTS)


def spread(ins, outs, send, recv, local, me, other, halves_in, halves_out, half_send, half_recv):
    for at in range(len(halves_in)):
        remote(
            halves_in[at], halves_out[at], half_send.at[at], half_recv.at[at], {"dp": other}
        ).start()
    for at in range(len(ins)):
        pltpu.make_async_copy(ins[at].at[me], outs[at].at[me], local.at[at]).start()

        @pl.loop(1, EXPERTS)
        def _(step):
            peer = peer_of(me, step)
            remote(
                ins[at].at[peer],
                outs[at].at[me],
                send.at[at, step],
                recv.at[at, step],
                {"expert": peer},
            ).start()


def settle(ins, outs, send, recv, local, me, other, halves_in, halves_out, half_send, half_recv):
    for at in range(len(ins)):
        pltpu.make_async_copy(ins[at].at[me], outs[at].at[me], local.at[at]).wait()

        @pl.loop(1, EXPERTS)
        def _(step):
            peer = peer_of(me, step)
            remote(
                ins[at].at[peer],
                outs[at].at[me],
                send.at[at, step],
                recv.at[at, step],
                {"expert": peer},
            ).wait()

    for at in range(len(halves_in)):
        remote(
            halves_in[at], halves_out[at], half_send.at[at], half_recv.at[at], {"dp": other}
        ).wait()


def dispatch_kernel(*refs):
    ins, halves_in = refs[0:3], refs[3:6]
    outs, halves_out = refs[6:9], refs[9:12]
    send, recv, local, half_send, half_recv = refs[12:]
    me = lax.axis_index("expert")
    other = 1 - lax.axis_index("dp")
    enter(me, other)
    moves = (ins, outs, send, recv, local, me, other, halves_in, halves_out, half_send, half_recv)
    spread(*moves)
    settle(*moves)


def collect_kernel(*refs):
    ins, halves_in, vec = refs[0:2], refs[2:5], refs[5]
    outs, halves_out, vec_out = refs[6:8], refs[8:11], refs[11]
    (
        send,
        recv,
        local,
        half_send,
        half_recv,
        vec_other,
        vec_sum,
        pair_sems,
        vec_send,
        vec_recv,
    ) = refs[12:]
    me = lax.axis_index("expert")
    other = 1 - lax.axis_index("dp")
    enter(me, other)
    pair = remote(vec, vec_other, pair_sems.at[0], pair_sems.at[1], {"dp": other})
    pair.start()
    moves = (ins, outs, send, recv, local, me, other, halves_in, halves_out, half_send, half_recv)
    spread(*moves)
    pair.wait()
    vec_sum[...] = vec[...] + vec_other[...]
    vec_out[me] = vec_sum[...]

    @pl.loop(1, EXPERTS)
    def _(step):
        remote(
            vec_sum,
            vec_out.at[me],
            vec_send.at[step],
            vec_recv.at[step],
            {"expert": peer_of(me, step)},
        ).start()

    @pl.loop(1, EXPERTS)
    def _(step):
        remote(
            vec_sum,
            vec_out.at[me],
            vec_send.at[step],
            vec_recv.at[step],
            {"expert": peer_of(me, step)},
        ).wait()

    settle(*moves)


def like(arrays):
    return [jax.ShapeDtypeStruct(a.shape, a.dtype) for a in arrays]


def dispatch(blocks, halves):
    hbm = pl.BlockSpec(memory_space=pl.ANY)
    dma = pltpu.SemaphoreType.DMA
    outs = pl.pallas_call(
        dispatch_kernel,
        out_shape=like(blocks) + like(halves),
        in_specs=[hbm] * 6,
        out_specs=[hbm] * 6,
        scratch_shapes=[dma((3, EXPERTS)), dma((3, EXPERTS)), dma((3,)), dma((3,)), dma((3,))],
        compiler_params=pltpu.CompilerParams(collective_id=0, has_side_effects=True),
        name="dispatch",
    )(*blocks, *halves)
    return outs[0:3], outs[3:6]


def collect(blocks, halves, vec):
    hbm = pl.BlockSpec(memory_space=pl.ANY)
    vmem = pl.BlockSpec(memory_space=pltpu.VMEM)
    dma = pltpu.SemaphoreType.DMA
    outs = pl.pallas_call(
        collect_kernel,
        out_shape=like(blocks)
        + like(halves)
        + [jax.ShapeDtypeStruct((EXPERTS,) + vec.shape, vec.dtype)],
        in_specs=[hbm] * 5 + [vmem],
        out_specs=[hbm] * 5 + [vmem],
        scratch_shapes=[
            dma((2, EXPERTS)),
            dma((2, EXPERTS)),
            dma((2,)),
            dma((3,)),
            dma((3,)),
            pltpu.VMEM(vec.shape, vec.dtype),
            pltpu.VMEM(vec.shape, vec.dtype),
            dma((2,)),
            dma((EXPERTS,)),
            dma((EXPERTS,)),
        ],
        compiler_params=pltpu.CompilerParams(collective_id=1, has_side_effects=True),
        name="collect",
    )(*blocks, *halves, vec)
    return outs[0:2], outs[2:5], outs[5]


def dot(left, right, left_dim=1, right_dim=0):
    return lax.dot_general(
        left, right, (((left_dim,), (right_dim,)), ((), ())), preferred_element_type=F32
    )


def norm_rows(inputs, gain_row):
    as_float = inputs.astype(F32)
    inverse = lax.rsqrt(jnp.mean(as_float * as_float, axis=-1, keepdims=True) + EPS)
    normed = (as_float * inverse * gain_row).astype(BF16)
    return as_float, inverse, normed


def placing(routes):
    tokens = routes.shape[0]
    lanes = lax.broadcasted_iota(jnp.int32, (tokens, EXPERTS), 1)
    named = (routes[:, 0:1] == lanes) | (routes[:, 1:2] == lanes)
    earlier = (
        lax.broadcasted_iota(jnp.int32, (tokens, tokens), 1)
        < lax.broadcasted_iota(jnp.int32, (tokens, tokens), 0)
    ).astype(BF16)
    before = dot(earlier, named.astype(BF16))
    slots = jnp.where(named, before, -1.0).astype(BF16)
    rows = EXPERTS * BLOCK
    row = lax.broadcasted_iota(jnp.int32, (rows, EXPERTS), 0)
    repeat = (row // BLOCK == lax.broadcasted_iota(jnp.int32, (rows, EXPERTS), 1)).astype(BF16)
    wide = dot(repeat, slots, 1, 1)
    wide = jnp.concatenate([wide] * QUARTS, axis=1)
    shape = (rows, QUARTS * tokens)
    row = lax.broadcasted_iota(jnp.int32, shape, 0)
    quarter = lax.broadcasted_iota(jnp.int32, shape, 1) // tokens
    same = (row // 4) % 4 == quarter
    slot = (row % 4).astype(F32)
    return [
        ((wide == slot + 4.0 * group) & same).astype(BF16) for group in range(GROUPS)
    ]


def tall(rows):
    return jnp.concatenate(
        [rows[:, q * SLAB : (q + 1) * SLAB] for q in range(QUARTS)], axis=0
    )


def broad(stacked):
    tokens = stacked.shape[0] // QUARTS
    return jnp.concatenate(
        [stacked[q * tokens : (q + 1) * tokens] for q in range(QUARTS)], axis=1
    )


def pack(places, rows):
    stacked = tall(rows)
    packed = jnp.concatenate([dot(place, stacked).astype(BF16) for place in places], axis=1)
    return packed.reshape(EXPERTS, BLOCK, GROUPS * SLAB)


def combine(places, returned):
    flat = returned.reshape(EXPERTS * BLOCK, GROUPS * SLAB)
    total = dot(places[0], flat[:, 0:SLAB], 0, 0)
    for group in range(1, GROUPS):
        total = total + dot(places[group], flat[:, group * SLAB : (group + 1) * SLAB], 0, 0)
    return broad(total)


def shuffle():
    shape = (128, 128)
    row = lax.broadcasted_iota(jnp.int32, shape, 0)
    col = lax.broadcasted_iota(jnp.int32, shape, 1)
    quarter, source, slot = row // 32, (row // 4) % 8, row % 4
    return (col == source * BLOCK + quarter * 4 + slot).astype(BF16)


def unpack(received):
    flat = received.reshape(EXPERTS * BLOCK, GROUPS * SLAB)
    order = shuffle()
    parts = [dot(order, flat[at * 128 : (at + 1) * 128]).astype(BF16) for at in range(4)]
    return jnp.concatenate(
        [
            jnp.concatenate(
                [
                    part[q * 32 : (q + 1) * 32, group * SLAB : (group + 1) * SLAB]
                    for q in range(QUARTS)
                ],
                axis=1,
            )
            for group in range(GROUPS)
            for part in parts
        ],
        axis=0,
    )


def repack(rows):
    order = shuffle()
    parts = []
    for at in range(4):
        part = jnp.concatenate(
            [
                jnp.concatenate(
                    [
                        rows[
                            group * 128 + at * 32 : group * 128 + (at + 1) * 32,
                            q * SLAB : (q + 1) * SLAB,
                        ]
                        for q in range(QUARTS)
                    ],
                    axis=0,
                )
                for group in range(GROUPS)
            ],
            axis=1,
        )
        parts.append(dot(order, part, 0, 0).astype(BF16))
    return jnp.concatenate(parts, axis=0).reshape(EXPERTS, BLOCK, GROUPS * SLAB)


def forward_half(rows, gate, up, down):
    pre_gate = dot(rows, gate, 1, 1)
    hidden = (pre_gate * jax.nn.sigmoid(pre_gate) * dot(rows, up, 1, 1)).astype(BF16)
    return dot(hidden, down)


def backward_half(rows, scaled, gate, up, down):
    pre_gate, pre_up = dot(rows, gate, 1, 1), dot(rows, up, 1, 1)
    sigm = jax.nn.sigmoid(pre_gate)
    swish = pre_gate * sigm
    hidden = (swish * pre_up).astype(BF16)
    grad_hidden = dot(scaled, down, 1, 1)
    share = jnp.sum(hidden.astype(F32) * grad_hidden, axis=1, keepdims=True)
    grad_up = (grad_hidden * swish).astype(BF16)
    grad_gate = (grad_hidden * pre_up * sigm * (1.0 + pre_gate * (1.0 - sigm))).astype(BF16)
    grad_rows = dot(grad_gate, gate) + dot(grad_up, up)
    return (
        share,
        grad_rows,
        dot(grad_gate, rows, 0, 0),
        dot(grad_up, rows, 0, 0),
        dot(hidden, scaled, 0, 0),
    )


def shifted(value, axis, steps):
    count = lax.axis_size(axis)
    return lax.ppermute(value, axis, [(at, (at + steps) % count) for at in range(count)])


def shards(fwd_in, saved_in, out_grad, gain, router, w_gate, w_up, w_down, routes_fwd, routes_bwd):
    gain_row = gain[0].astype(F32)
    own = (w_gate[0, 0].T, w_up[0, 0].T, w_down[0, 0])
    me = lax.axis_index("expert")
    column = lax.broadcasted_iota(jnp.int32, router[0].shape, 1) == me
    mine = jnp.sum(jnp.where(column, router[0].astype(F32), 0.0), axis=1)

    x_fwd, _, normed_fwd = norm_rows(fwd_in[0], gain_row)
    places_fwd = placing(routes_fwd[0])
    x_bwd, inverse, normed_bwd = norm_rows(saved_in[0], gain_row)
    places_bwd = placing(routes_bwd[0])
    cot = out_grad[0].astype(F32)
    (rows_bwd, cot_rows, rows_fwd), far = dispatch(
        (
            pack(places_bwd, normed_bwd),
            pack(places_bwd, out_grad[0]),
            pack(places_fwd, normed_fwd),
        ),
        own,
    )

    rows_bwd, cot_rows, rows_fwd = unpack(rows_bwd), unpack(cot_rows), unpack(rows_fwd)

    def gates(rows):
        logits = jnp.sum(rows.astype(F32) * mine[None, :], axis=1, keepdims=True)
        return jax.nn.sigmoid(logits)

    gate_bwd = gates(rows_bwd)
    scaled = (gate_bwd * cot_rows.astype(F32)).astype(BF16)
    near_grads = backward_half(rows_bwd, scaled, *own)
    far_grads = backward_half(rows_bwd, scaled, *far)
    dlogit = ((near_grads[0] + far_grads[0]) * (1.0 - gate_bwd)).astype(BF16).astype(F32)
    grad_rows = near_grads[1] + far_grads[1] + dlogit * mine[None, :]
    rows_float = rows_bwd.astype(F32)
    router_column = jnp.sum(rows_float * dlogit, axis=0)
    gain_part = jnp.sum(rows_float * grad_rows, axis=0) / gain_row
    vec = jnp.concatenate([router_column.reshape(16, 128), gain_part.reshape(16, 128)], axis=0)
    result = gates(rows_fwd) * (forward_half(rows_fwd, *own) + forward_half(rows_fwd, *far))

    (rows_back, result_back), partner, vecs = collect(
        (repack(grad_rows.astype(BF16)), repack(result.astype(BF16))),
        tuple(grad.astype(BF16) for grad in far_grads[2:]),
        vec,
    )
    mixed = (x_fwd + combine(places_fwd, result_back)).astype(BF16)
    sent_fwd = shifted(mixed[None], "section", 1)
    dnormed = combine(places_bwd, rows_back)
    scaled_grad = dnormed * gain_row
    in_grad = cot + inverse * scaled_grad
    in_grad = in_grad - x_bwd * inverse**3 * jnp.mean(
        scaled_grad * x_bwd, axis=-1, keepdims=True
    )
    sent_bwd = shifted(in_grad.astype(BF16)[None], "section", -1)
    totals = [
        (near + there.astype(F32)).astype(BF16)
        for near, there in zip(near_grads[2:], partner, strict=True)
    ]
    totals = [total[None, None] for total in (totals[0].T, totals[1].T, totals[2])]
    model_width = fwd_in.shape[2]
    grad_router = vecs[:, 0:16].reshape(EXPERTS, model_width).T
    grad_gain = jnp.sum(vecs[:, 16:32], axis=0).reshape(model_width)
    return (sent_fwd, sent_bwd, *totals, grad_router[None], grad_gain[None])


def solution(mesh):
    tokens = P("section", ("expert", "dp"), None)
    wide = P("section", "expert", None, "dp")
    deep = P("section", "expert", "dp", None)
    gain, router = P("section", None), P("section", None, None)
    return jax.shard_map(
        shards,
        mesh=mesh,
        in_specs=(tokens, tokens, tokens, gain, router, wide, wide, deep, tokens, tokens),
        out_specs=(tokens, tokens, wide, wide, deep, router, gain),
        check_vma=False,
    )
```

```python
import jax
import jax.numpy as jnp
from jax import lax
from jax.experimental import pallas as pl
from jax.experimental.pallas import tpu as pltpu
from jax.sharding import PartitionSpec as P

EPS = 1e-06
MESH = pl.DeviceIdType.MESH
EXPERTS = 32
CAP = 12
GROUPS = 3
QUARTS = 4
SLAB = 512
BLOCK = 16
F32 = jnp.float32
BF16 = jnp.bfloat16


def peer_of(me, step):
    return lax.rem(me // 4 + step // 4, 8) * 4 + lax.rem(me + step, 4)


def remote(src, dst, send_sem, recv_sem, device):
    return pltpu.make_async_remote_copy(
        src_ref=src,
        dst_ref=dst,
        send_sem=send_sem,
        recv_sem=recv_sem,
        device_id=device,
        device_id_type=MESH,
    )


def dot(left, right, left_dim=1, right_dim=0):
    return lax.dot_general(
        left, right, (((left_dim,), (right_dim,)), ((), ())), preferred_element_type=F32
    )


def norm_rows(inputs, gain_row):
    as_float = inputs.astype(F32)
    inverse = lax.rsqrt(jnp.mean(as_float * as_float, axis=-1, keepdims=True) + EPS)
    normed = (as_float * inverse * gain_row).astype(BF16)
    return as_float, inverse, normed


def place(places, routes):
    tokens = routes.shape[0]
    lanes = lax.broadcasted_iota(jnp.int32, (tokens, EXPERTS), 1)
    named = (routes[:, 0:1] == lanes) | (routes[:, 1:2] == lanes)
    earlier = (
        lax.broadcasted_iota(jnp.int32, (tokens, tokens), 1)
        < lax.broadcasted_iota(jnp.int32, (tokens, tokens), 0)
    ).astype(F32)
    before = dot(earlier.astype(BF16), named.astype(F32).astype(BF16))
    slots = jnp.where(named, before, -1.0).astype(BF16)
    rows = EXPERTS * BLOCK
    row = lax.broadcasted_iota(jnp.int32, (rows, EXPERTS), 0)
    repeat = (row >> 4) == lax.broadcasted_iota(jnp.int32, (rows, EXPERTS), 1)
    wide = dot(repeat.astype(F32).astype(BF16), slots, 1, 1)
    row = lax.broadcasted_iota(jnp.int32, (rows, tokens), 0)
    quarter = (row >> 2) & 3
    slot = (row & 3).astype(F32)
    for group in range(GROUPS):
        hit = jnp.where(wide == slot + 4.0 * group, 1.0, 0.0)
        for q in range(QUARTS):
            places[group, :, q * tokens : (q + 1) * tokens] = jnp.where(
                quarter == q, hit, 0.0
            ).astype(BF16)


def pack(places, rows, packed):
    stacked = jnp.concatenate(
        [rows[:, q * SLAB : (q + 1) * SLAB] for q in range(QUARTS)], axis=0
    )
    for group in range(GROUPS):
        packed[:, group * SLAB : (group + 1) * SLAB] = dot(places[group], stacked).astype(BF16)


def combine(places, returned):
    total = dot(places[0], returned[:, 0:SLAB], 0, 0)
    for group in range(1, GROUPS):
        total = total + dot(places[group], returned[:, group * SLAB : (group + 1) * SLAB], 0, 0)
    tokens = total.shape[0] // QUARTS
    return jnp.concatenate(
        [total[q * tokens : (q + 1) * tokens] for q in range(QUARTS)], axis=1
    )


def shuffle():
    row = lax.broadcasted_iota(jnp.int32, (128, 128), 0)
    col = lax.broadcasted_iota(jnp.int32, (128, 128), 1)
    wanted = (((row >> 2) & 7) << 4) + ((row >> 5) << 2) + (row & 3)
    return jnp.where(col == wanted, 1.0, 0.0).astype(BF16)


def unpack(received, rows):
    order = shuffle()
    for at in range(4):
        part = dot(order, received[at * 128 : (at + 1) * 128, :]).astype(BF16)
        for group in range(GROUPS):
            for q in range(QUARTS):
                rows[
                    group * 128 + at * 32 : group * 128 + (at + 1) * 32,
                    q * SLAB : (q + 1) * SLAB,
                ] = part[q * 32 : (q + 1) * 32, group * SLAB : (group + 1) * SLAB]


def repack(rows, packed):
    order = shuffle()
    for at in range(4):
        for group in range(GROUPS):
            part = jnp.concatenate(
                [
                    rows[
                        group * 128 + at * 32 : group * 128 + (at + 1) * 32,
                        q * SLAB : (q + 1) * SLAB,
                    ]
                    for q in range(QUARTS)
                ],
                axis=0,
            ).astype(BF16)
            packed[at * 128 : (at + 1) * 128, group * SLAB : (group + 1) * SLAB] = dot(
                order, part, 0, 0
            ).astype(BF16)


def slabs():
    def over(body):
        @pl.loop(0, QUARTS)
        def _(q):
            body(pl.ds(pl.multiple_of(q * SLAB, SLAB), SLAB))

    return over


def backward_half(rows, scaled, weights, hidden, grad_gate, grad_up, grad_rows, add):
    gate, up, down = weights
    pre_gate, pre_up = dot(rows[...], gate[...], 1, 1), dot(rows[...], up[...], 1, 1)
    grad_hidden = dot(scaled[...], down[...], 1, 1)
    sigm = jax.nn.sigmoid(pre_gate)
    swish = pre_gate * sigm
    hidden[...] = (swish * pre_up).astype(BF16)
    share = jnp.sum(hidden[...].astype(F32) * grad_hidden, axis=1, keepdims=True)
    grad_up[...] = (grad_hidden * swish).astype(BF16)
    grad_gate[...] = (
        grad_hidden * pre_up * sigm * (1.0 + pre_gate * (1.0 - sigm))
    ).astype(BF16)

    @slabs()
    def _(cols):
        part = dot(grad_gate[...], gate[:, cols]) + dot(grad_up[...], up[:, cols])
        grad_rows[:, cols] = grad_rows[:, cols] + part if add else part

    return share


def weight_grad(left, right, target, addend):
    turned = left[...].T

    @slabs()
    def _(cols):
        part = dot(turned, right[:, cols])
        if addend is not None:
            part = part + addend[:, cols].astype(F32)
        target[:, cols] = part.astype(BF16)


def relay_kernel(*refs):
    (
        fwd_in,
        saved_in,
        out_grad,
        gain,
        router,
        w_gate,
        w_up,
        w_down,
        routes_fwd,
        routes_bwd,
        sent_fwd,
        sent_bwd,
        total_gate,
        total_up,
        total_down,
        router_total,
        gain_total,
        places_fwd,
        places_bwd,
        out_blocks,
        in_blocks,
        rows,
        scaled,
        rows_fwd,
        far,
        hidden,
        grad_gate,
        grad_up,
        fwd_hidden,
        grad_rows,
        far_grads,
        there_grads,
        back_out,
        back_in,
        shift_out,
        vec,
        vec_other,
        vec_sum,
        vecs,
        out_send,
        out_recv,
        back_send,
        back_recv,
        local,
        far_send,
        far_recv,
        grad_send,
        grad_recv,
        shift_send,
        shift_recv,
        pair_sems,
        vec_send,
        vec_recv,
    ) = refs
    me = lax.axis_index("expert")
    other = {"dp": 1 - lax.axis_index("dp")}
    section = lax.axis_index("section")
    after = {"section": lax.rem(section + 1, 4)}
    ahead = {"section": lax.rem(section + 3, 4)}
    own = (w_gate, w_up, w_down)
    fars = tuple(far.at[at] for at in range(3))

    barrier = pltpu.get_barrier_semaphore()

    @pl.loop(1, EXPERTS)
    def _(step):
        pl.semaphore_signal(
            barrier, inc=1, device_id={"expert": peer_of(me, step)}, device_id_type=MESH
        )

    for device in (other, after, ahead):
        pl.semaphore_signal(barrier, inc=1, device_id=device, device_id_type=MESH)

    def block(of):
        return pl.ds(pl.multiple_of(of * BLOCK, BLOCK), BLOCK)

    def each(sources, targets, send, recv, act):
        @pl.loop(1, EXPERTS)
        def _(step):
            peer = peer_of(me, step)
            act(
                remote(
                    sources.at[block(peer)],
                    targets.at[block(me)],
                    send.at[step],
                    recv.at[step],
                    {"expert": peer},
                )
            )

    def own_block(sources, targets, sem):
        return pltpu.make_async_copy(sources.at[block(me)], targets.at[block(me)], sem)

    def issue(sources, targets, send, recv, sem):
        own_block(sources, targets, sem).start()
        each(sources, targets, send, recv, lambda copy: copy.start())

    def arrive(sources, targets, send, recv, sem):
        own_block(sources, targets, sem).wait()
        each(sources, targets, send, recv, lambda copy: copy.wait())

    def outward(at):
        return (
            out_blocks.at[at], in_blocks.at[at], out_send.at[at], out_recv.at[at], local.at[at],
        )

    def homeward(at):
        return (
            back_out.at[at], back_in.at[at], back_send.at[at], back_recv.at[at], local.at[3 + at],
        )

    gain_row = gain[...].astype(F32)
    place(places_bwd, routes_bwd[...])
    normed = norm_rows(saved_in[...], gain_row)[2]
    pack(places_bwd, normed, out_blocks.at[0])

    pl.semaphore_wait(barrier, EXPERTS + 2)
    issue(*outward(0))
    weight_moves = [
        remote(own[at], fars[at], far_send.at[at], far_recv.at[at], other) for at in range(3)
    ]
    for move in weight_moves:
        move.start()
    pack(places_bwd, out_grad[...], out_blocks.at[1])
    issue(*outward(1))
    place(places_fwd, routes_fwd[...])
    normed = norm_rows(fwd_in[...], gain_row)[2]
    pack(places_fwd, normed, out_blocks.at[2])

    lanes = lax.broadcasted_iota(jnp.int32, (rows.shape[0], EXPERTS), 1)

    def gates(of):
        logits = dot(of[...], router[...], 1, 1)
        return jax.nn.sigmoid(jnp.sum(jnp.where(lanes == me, logits, 0.0), axis=1, keepdims=True))

    arrive(*outward(0))
    issue(*outward(2))
    unpack(in_blocks.at[0], rows)
    gate_bwd = gates(rows)
    arrive(*outward(1))
    unpack(in_blocks.at[1], scaled)

    @slabs()
    def _(cols):
        scaled[:, cols] = (gate_bwd * scaled[:, cols].astype(F32)).astype(BF16)

    def half(weights, at, add):
        return backward_half(
            rows, scaled, weights, hidden.at[at], grad_gate.at[at], grad_up.at[at], grad_rows, add
        )

    share = half(own, 0, False)
    for move in weight_moves:
        move.wait()
    share = share + half(fars, 1, True)
    grad_moves = [
        remote(
            far_grads.at[at], there_grads.at[at], grad_send.at[at], grad_recv.at[at], other
        )
        for at in range(3)
    ]

    factors = ((grad_gate, rows), (grad_up, rows), (hidden, scaled))
    for at, (left, right) in enumerate(factors):
        weight_grad(left.at[1], right, far_grads.at[at], None)
        grad_moves[at].start()

    dlogit = (share * (1.0 - gate_bwd)).astype(BF16).astype(F32)
    row = lax.broadcasted_iota(jnp.int32, router.shape, 0)
    mine = jnp.sum(jnp.where(row == me, router[...].astype(F32), 0.0), axis=0, keepdims=True)
    for q in range(QUARTS):
        cols = slice(q * SLAB, (q + 1) * SLAB)
        part = grad_rows[:, cols] + dlogit * mine[:, cols]
        grad_rows[:, cols] = part
        rows_float = rows[:, cols].astype(F32)
        router_column = jnp.sum(rows_float * dlogit, axis=0, keepdims=True)
        gain_part = jnp.sum(rows_float * part, axis=0, keepdims=True) / gain_row[:, cols]
        for at in range(4):
            vec[q * 4 + at : q * 4 + at + 1, :] = router_column[:, at * 128 : (at + 1) * 128]
            vec[16 + q * 4 + at : 17 + q * 4 + at, :] = gain_part[:, at * 128 : (at + 1) * 128]
    repack(grad_rows, back_out.at[0])
    issue(*homeward(0))
    pair = remote(vec, vec_other, pair_sems.at[0], pair_sems.at[1], other)
    pair.start()

    arrive(*outward(2))
    unpack(in_blocks.at[2], rows_fwd)
    gate_fwd = gates(rows_fwd)
    for at, (gate, up, down) in enumerate((own, fars)):
        pre_gate, pre_up = dot(rows_fwd[...], gate[...], 1, 1), dot(rows_fwd[...], up[...], 1, 1)
        fwd_hidden[...] = (pre_gate * jax.nn.sigmoid(pre_gate) * pre_up).astype(BF16)

        @slabs()
        def _(cols):
            part = gate_fwd * dot(fwd_hidden[...], down[:, cols])
            grad_rows[:, cols] = grad_rows[:, cols] + part if at else part

    repack(grad_rows, back_out.at[1])
    issue(*homeward(1))

    pair.wait()
    vec_sum[...] = vec[...] + vec_other[...]
    vecs[me] = vec_sum[...]

    def share_vec(act):
        @pl.loop(1, EXPERTS)
        def _(step):
            act(
                remote(
                    vec_sum,
                    vecs.at[me],
                    vec_send.at[step],
                    vec_recv.at[step],
                    {"expert": peer_of(me, step)},
                )
            )

    share_vec(lambda copy: copy.start())

    arrive(*homeward(0))
    dnormed = combine(places_bwd, back_in.at[0])
    x_bwd, inverse, _ = norm_rows(saved_in[...], gain_row)
    scaled_grad = dnormed * gain_row
    mean = jnp.mean(scaled_grad * x_bwd, axis=-1, keepdims=True)
    in_grad = out_grad[...].astype(F32) + inverse * scaled_grad - x_bwd * inverse**3 * mean
    shift_out[0] = in_grad.astype(BF16)
    shift_bwd = remote(shift_out.at[0], sent_bwd, shift_send.at[0], shift_recv.at[0], ahead)
    shift_bwd.start()

    arrive(*homeward(1))
    mixed = fwd_in[...].astype(F32) + combine(places_fwd, back_in.at[1])
    shift_out[1] = mixed.astype(BF16)
    shift_fwd = remote(shift_out.at[1], sent_fwd, shift_send.at[1], shift_recv.at[1], after)
    shift_fwd.start()

    share_vec(lambda copy: copy.wait())
    gain_total[...] = jnp.sum(vecs[:, 16:32, :], axis=0)
    for at in range(16):
        router_total[:, at * 128 : (at + 1) * 128] = vecs[:, at, :]

    totals = (total_gate, total_up, total_down)
    for at, (left, right) in enumerate(factors):
        grad_moves[at].wait()
        weight_grad(left.at[0], right, totals[at], there_grads.at[at])
    shift_bwd.wait()
    shift_fwd.wait()


def relay(*operands):
    fwd_in, router, w_down = operands[0], operands[4], operands[7]
    tokens, width = fwd_in.shape
    half = w_down.shape[0]
    packed = (EXPERTS * BLOCK, GROUPS * SLAB)
    pairs = EXPERTS * CAP
    vmem = pl.BlockSpec(memory_space=pltpu.VMEM)
    dma = pltpu.SemaphoreType.DMA
    out_shape = [
        jax.ShapeDtypeStruct((tokens, width), BF16),
        jax.ShapeDtypeStruct((tokens, width), BF16),
        jax.ShapeDtypeStruct((half, width), BF16),
        jax.ShapeDtypeStruct((half, width), BF16),
        jax.ShapeDtypeStruct((half, width), BF16),
        jax.ShapeDtypeStruct((EXPERTS, width), F32),
        jax.ShapeDtypeStruct((16, 128), F32),
    ]
    scratch = [
        pltpu.VMEM((GROUPS, packed[0], QUARTS * tokens), BF16),
        pltpu.VMEM((GROUPS, packed[0], QUARTS * tokens), BF16),
        pltpu.VMEM((3,) + packed, BF16),
        pltpu.VMEM((3,) + packed, BF16),
        pltpu.VMEM((pairs, width), BF16),
        pltpu.VMEM((pairs, width), BF16),
        pltpu.VMEM((pairs, width), BF16),
        pltpu.VMEM((3, half, width), BF16),
        pltpu.VMEM((2, pairs, half), BF16),
        pltpu.VMEM((2, pairs, half), BF16),
        pltpu.VMEM((2, pairs, half), BF16),
        pltpu.VMEM((pairs, half), BF16),
        pltpu.VMEM((pairs, width), F32),
        pltpu.VMEM((3, half, width), BF16),
        pltpu.VMEM((3, half, width), BF16),
        pltpu.VMEM((2,) + packed, BF16),
        pltpu.VMEM((2,) + packed, BF16),
        pltpu.VMEM((2, tokens, width), BF16),
        pltpu.VMEM((32, 128), F32),
        pltpu.VMEM((32, 128), F32),
        pltpu.VMEM((32, 128), F32),
        pltpu.VMEM((EXPERTS, 32, 128), F32),
        dma((3, EXPERTS)),
        dma((3, EXPERTS)),
        dma((2, EXPERTS)),
        dma((2, EXPERTS)),
        dma((5,)),
        dma((3,)),
        dma((3,)),
        dma((3,)),
        dma((3,)),
        dma((2,)),
        dma((2,)),
        dma((2,)),
        dma((EXPERTS,)),
        dma((EXPERTS,)),
    ]
    return pl.pallas_call(
        relay_kernel,
        out_shape=out_shape,
        in_specs=[vmem] * len(operands),
        out_specs=[vmem] * len(out_shape),
        scratch_shapes=scratch,
        compiler_params=pltpu.CompilerParams(
            collective_id=0, has_side_effects=True, vmem_limit_bytes=63 << 20
        ),
        name="relay",
    )(*operands)


def shards(fwd_in, saved_in, out_grad, gain, router, w_gate, w_up, w_down, routes_fwd, routes_bwd):
    sent_fwd, sent_bwd, total_gate, total_up, total_down, router_total, gain_total = relay(
        fwd_in[0],
        saved_in[0],
        out_grad[0],
        gain,
        router[0].T,
        w_gate[0, 0].T,
        w_up[0, 0].T,
        w_down[0, 0],
        routes_fwd[0],
        routes_bwd[0],
    )
    return (
        sent_fwd[None],
        sent_bwd[None],
        total_gate.T[None, None],
        total_up.T[None, None],
        total_down[None, None],
        router_total.T[None],
        gain_total.reshape(1, -1),
    )


def solution(mesh):
    tokens = P("section", ("expert", "dp"), None)
    wide = P("section", "expert", None, "dp")
    deep = P("section", "expert", "dp", None)
    gain, router = P("section", None), P("section", None, None)
    return jax.shard_map(
        shards,
        mesh=mesh,
        in_specs=(tokens, tokens, tokens, gain, router, wide, wide, deep, tokens, tokens),
        out_specs=(tokens, tokens, wide, wide, deep, router, gain),
        check_vma=False,
    )
```

```python
import jax
import jax.numpy as jnp
from jax import lax
from jax.experimental import pallas as pl
from jax.experimental.pallas import tpu as pltpu
from jax.sharding import PartitionSpec as P

EPS = 1e-06
MESH = pl.DeviceIdType.MESH
EXPERTS = 32
CAP = 12
GROUPS = 3
QUARTS = 4
SLAB = 512
BLOCK = 16
FIRST = 256
F32 = jnp.float32
BF16 = jnp.bfloat16


def peer_of(me, step):
    return lax.rem(me // 4 + step // 4, 8) * 4 + lax.rem(me + step, 4)


def remote(src, dst, send_sem, recv_sem, device):
    return pltpu.make_async_remote_copy(
        src_ref=src,
        dst_ref=dst,
        send_sem=send_sem,
        recv_sem=recv_sem,
        device_id=device,
        device_id_type=MESH,
    )


def dot(left, right, left_dim=1, right_dim=0):
    return lax.dot_general(
        left, right, (((left_dim,), (right_dim,)), ((), ())), preferred_element_type=F32
    )


def norm_rows(inputs, gain_row):
    as_float = inputs.astype(F32)
    inverse = lax.rsqrt(jnp.mean(as_float * as_float, axis=-1, keepdims=True) + EPS)
    normed = (as_float * inverse * gain_row).astype(BF16)
    return as_float, inverse, normed


def place(places, routes):
    tokens = routes.shape[1]
    experts = lax.broadcasted_iota(jnp.int32, (EXPERTS, tokens), 0)
    named = (routes[0:1, :] == experts) | (routes[1:2, :] == experts)
    earlier = (
        lax.broadcasted_iota(jnp.int32, (tokens, tokens), 0)
        < lax.broadcasted_iota(jnp.int32, (tokens, tokens), 1)
    ).astype(F32)
    before = dot(named.astype(F32).astype(BF16), earlier.astype(BF16))
    slots = jnp.where(named, before, -1.0).astype(BF16)
    rows = EXPERTS * BLOCK
    row = lax.broadcasted_iota(jnp.int32, (rows, EXPERTS), 0)
    repeat = (row >> 4) == lax.broadcasted_iota(jnp.int32, (rows, EXPERTS), 1)
    wide = dot(repeat.astype(F32).astype(BF16), slots)
    row = lax.broadcasted_iota(jnp.int32, (rows, tokens), 0)
    quarter = (row >> 2) & 3
    slot = (row & 3).astype(F32)
    for group in range(GROUPS):
        hit = jnp.where(wide == slot + 4.0 * group, 1.0, 0.0)
        for q in range(QUARTS):
            places[group, :, q * tokens : (q + 1) * tokens] = jnp.where(
                quarter == q, hit, 0.0
            ).astype(BF16)


def pack(places, rows, packed):
    stacked = jnp.concatenate(
        [rows[:, q * SLAB : (q + 1) * SLAB] for q in range(QUARTS)], axis=0
    )
    for group in range(GROUPS):
        packed[:, group * SLAB : (group + 1) * SLAB] = dot(places[group], stacked).astype(BF16)


def combine(places, returned):
    total = dot(places[0], returned[:, 0:SLAB], 0, 0)
    for group in range(1, GROUPS):
        total = total + dot(places[group], returned[:, group * SLAB : (group + 1) * SLAB], 0, 0)
    tokens = total.shape[0] // QUARTS
    return jnp.concatenate(
        [total[q * tokens : (q + 1) * tokens] for q in range(QUARTS)], axis=1
    )


def shuffle():
    row = lax.broadcasted_iota(jnp.int32, (128, 128), 0)
    col = lax.broadcasted_iota(jnp.int32, (128, 128), 1)
    wanted = (((row >> 2) & 7) << 4) + ((row >> 5) << 2) + (row & 3)
    return jnp.where(col == wanted, 1.0, 0.0).astype(BF16)


def unpack(received, rows):
    order = shuffle()
    for at in range(4):
        part = dot(order, received[at * 128 : (at + 1) * 128, :]).astype(BF16)
        for group in range(GROUPS):
            for q in range(QUARTS):
                rows[
                    group * 128 + at * 32 : group * 128 + (at + 1) * 32,
                    q * SLAB : (q + 1) * SLAB,
                ] = part[q * 32 : (q + 1) * 32, group * SLAB : (group + 1) * SLAB]


def repack(rows, packed):
    order = shuffle()
    for at in range(4):
        for group in range(GROUPS):
            part = jnp.concatenate(
                [
                    rows[
                        group * 128 + at * 32 : group * 128 + (at + 1) * 32,
                        q * SLAB : (q + 1) * SLAB,
                    ]
                    for q in range(QUARTS)
                ],
                axis=0,
            ).astype(BF16)
            packed[at * 128 : (at + 1) * 128, group * SLAB : (group + 1) * SLAB] = dot(
                order, part, 0, 0
            ).astype(BF16)


def slabs():
    def over(body):
        @pl.loop(0, QUARTS)
        def _(q):
            body(pl.ds(pl.multiple_of(q * SLAB, SLAB), SLAB))

    return over


def pre_activate(rows, piece):
    piece.pre_gate[...] = dot(rows[...], piece.gate[...], 1, 1)
    piece.pre_up[...] = dot(rows[...], piece.up[...], 1, 1)


def backward_piece(scaled, piece):
    grad_hidden = dot(scaled[...], piece.down[...], 1, 1)
    pre_gate, pre_up = piece.pre_gate[...], piece.pre_up[...]
    sigm = jax.nn.sigmoid(pre_gate)
    swish = pre_gate * sigm
    hidden = (swish * pre_up).astype(BF16)
    piece.hidden[...] = hidden
    piece.grad_up[...] = (grad_hidden * swish).astype(BF16)
    piece.grad_gate[...] = (
        grad_hidden * pre_up * sigm * (1.0 + pre_gate * (1.0 - sigm))
    ).astype(BF16)
    return jnp.sum(hidden.astype(F32) * grad_hidden, axis=1, keepdims=True)


def row_grads(piece, grad_rows, add):
    @slabs()
    def _(cols):
        part = dot(piece.grad_gate[...], piece.gate[:, cols])
        part = part + dot(piece.grad_up[...], piece.up[:, cols])
        grad_rows[:, cols] = grad_rows[:, cols] + part if add else part


def weight_grad(left, right, target, addend):
    turned = left[...].T

    @slabs()
    def _(cols):
        part = dot(turned, right[:, cols])
        if addend is not None:
            part = part + addend[:, cols].astype(F32)
        target[:, cols] = part.astype(target.dtype)


class Piece:
    def __init__(self, weights, kept):
        self.gate, self.up, self.down = weights
        self.pre_gate, self.pre_up, self.hidden, self.grad_gate, self.grad_up = kept


def relay_kernel(*refs):
    refs = list(refs)

    def take(count):
        taken = refs[:count]
        del refs[:count]
        return taken

    fwd_in, saved_in, out_grad, gain, router = take(5)
    own_hbm = take(3)
    routes_fwd, routes_bwd = take(2)
    sent_fwd, sent_bwd = take(2)
    totals = take(3)
    router_total, gain_total = take(2)
    places_fwd, places_bwd, out_blocks, in_blocks, rows, scaled, rows_fwd, near, far = take(9)
    kept_near, kept_first, kept_last = take(5), take(5), take(5)
    fwd_hidden, grad_rows, far_grads, there_grads, back_out, back_in, shift_out = take(7)
    near_last = take(1)[0]
    vec, vec_other, vec_sum, vecs = take(4)
    out_send, out_recv, back_send, back_recv, local = take(5)
    near_sems, far_send, far_recv, grad_send, grad_recv, total_sems = take(6)
    shift_send, shift_recv, pair_sems, vec_send, vec_recv = take(5)

    me = lax.axis_index("expert")
    other = {"dp": 1 - lax.axis_index("dp")}
    section = lax.axis_index("section")
    after = {"section": lax.rem(section + 1, 4)}
    ahead = {"section": lax.rem(section + 3, 4)}
    half = near.shape[1]
    cuts = (slice(0, FIRST), slice(FIRST, half))

    barrier = pltpu.get_barrier_semaphore()

    @pl.loop(1, EXPERTS)
    def _(step):
        pl.semaphore_signal(
            barrier, inc=1, device_id={"expert": peer_of(me, step)}, device_id_type=MESH
        )

    for device in (other, after, ahead):
        pl.semaphore_signal(barrier, inc=1, device_id=device, device_id_type=MESH)

    near_moves = [
        pltpu.make_async_copy(own_hbm[at], near.at[at], near_sems.at[at]) for at in range(3)
    ]
    for move in near_moves:
        move.start()

    def block(of):
        return pl.ds(pl.multiple_of(of * BLOCK, BLOCK), BLOCK)

    def each(sources, targets, send, recv, act):
        @pl.loop(1, EXPERTS)
        def _(step):
            peer = peer_of(me, step)
            act(
                remote(
                    sources.at[block(peer)],
                    targets.at[block(me)],
                    send.at[step],
                    recv.at[step],
                    {"expert": peer},
                )
            )

    def own_block(sources, targets, sem):
        return pltpu.make_async_copy(sources.at[block(me)], targets.at[block(me)], sem)

    def issue(sources, targets, send, recv, sem):
        each(sources, targets, send, recv, lambda copy: copy.start())
        own_block(sources, targets, sem).start()

    def arrive(sources, targets, send, recv, sem):
        own_block(sources, targets, sem).wait()
        each(sources, targets, send, recv, lambda copy: copy.wait())

    def outward(at):
        return (
            out_blocks.at[at], in_blocks.at[at], out_send.at[at], out_recv.at[at], local.at[at],
        )

    def homeward(at):
        return (
            back_out.at[at], back_in.at[at], back_send.at[at], back_recv.at[at], local.at[3 + at],
        )

    weight_moves = [
        [
            remote(
                own_hbm[at].at[cut],
                far.at[at, cut],
                far_send.at[turn, at],
                far_recv.at[turn, at],
                other,
            )
            for at in range(3)
        ]
        for turn, cut in enumerate(cuts)
    ]
    grad_moves = [
        [
            remote(
                far_grads.at[at, cut],
                there_grads.at[at, cut],
                grad_send.at[turn, at],
                grad_recv.at[turn, at],
                other,
            )
            for at in range(3)
        ]
        for turn, cut in enumerate(cuts)
    ]
    total_moves = [
        [
            pltpu.make_async_copy(
                there_grads.at[at, cut], totals[at].at[cut], total_sems.at[turn, at]
            )
            for at in range(3)
        ]
        for turn, cut in enumerate(cuts)
    ]
    mine = Piece([near.at[at] for at in range(3)], kept_near)
    first = Piece([far.at[at, cuts[0]] for at in range(3)], kept_first)
    last = Piece([far.at[at, cuts[1]] for at in range(3)], kept_last)

    gain_row = gain[...].astype(F32)
    place(places_bwd, routes_bwd)
    normed = norm_rows(saved_in[...], gain_row)[2]
    pack(places_bwd, normed, out_blocks.at[0])

    pl.semaphore_wait(barrier, EXPERTS + 2)
    for move in weight_moves[0]:
        move.start()
    issue(*outward(0))
    for move in weight_moves[1]:
        move.start()
    pack(places_bwd, out_grad[...], out_blocks.at[1])
    issue(*outward(1))
    place(places_fwd, routes_fwd)
    normed = norm_rows(fwd_in[...], gain_row)[2]
    pack(places_fwd, normed, out_blocks.at[2])

    lanes = lax.broadcasted_iota(jnp.int32, (rows.shape[0], EXPERTS), 1)

    def gates(of):
        logits = dot(of[...], router[...], 1, 1)
        return jax.nn.sigmoid(jnp.sum(jnp.where(lanes == me, logits, 0.0), axis=1, keepdims=True))

    def send_grads(piece, turn):
        cut = cuts[turn]
        factors = ((piece.grad_gate, rows), (piece.grad_up, rows), (piece.hidden, scaled))
        for at, (left, right) in enumerate(factors):
            weight_grad(left, right, far_grads.at[at, cut], None)
            grad_moves[turn][at].start()

    arrive(*outward(0))
    issue(*outward(2))
    unpack(in_blocks.at[0], rows)
    gate_bwd = gates(rows)
    for move in near_moves:
        move.wait()
    pre_activate(rows, mine)
    for move in weight_moves[0]:
        move.wait()
    pre_activate(rows, first)

    arrive(*outward(1))
    unpack(in_blocks.at[1], scaled)

    @slabs()
    def _(cols):
        scaled[:, cols] = (gate_bwd * scaled[:, cols].astype(F32)).astype(BF16)

    share = backward_piece(scaled, first)
    send_grads(first, 0)
    share = share + backward_piece(scaled, mine)
    row_grads(first, grad_rows, False)
    row_grads(mine, grad_rows, True)
    for move in weight_moves[1]:
        move.wait()
    pre_activate(rows, last)
    share = share + backward_piece(scaled, last)
    send_grads(last, 1)
    row_grads(last, grad_rows, True)

    dlogit = (share * (1.0 - gate_bwd)).astype(BF16).astype(F32)
    row = lax.broadcasted_iota(jnp.int32, router.shape, 0)

    @slabs()
    def _(cols):
        part = dlogit * jnp.sum(
            jnp.where(row[:, 0:SLAB] == me, router[:, cols].astype(F32), 0.0),
            axis=0,
            keepdims=True,
        )
        grad_rows[:, cols] = grad_rows[:, cols] + part

    repack(grad_rows, back_out.at[0])
    issue(*homeward(0))
    for q in range(QUARTS):
        cols = slice(q * SLAB, (q + 1) * SLAB)
        rows_float = rows[:, cols].astype(F32)
        router_column = jnp.sum(rows_float * dlogit, axis=0, keepdims=True)
        gain_part = jnp.sum(rows_float * grad_rows[:, cols], axis=0, keepdims=True)
        gain_part = gain_part / gain_row[:, cols]
        for at in range(4):
            vec[q * 4 + at : q * 4 + at + 1, :] = router_column[:, at * 128 : (at + 1) * 128]
            vec[16 + q * 4 + at : 17 + q * 4 + at, :] = gain_part[:, at * 128 : (at + 1) * 128]
    pair = remote(vec, vec_other, pair_sems.at[0], pair_sems.at[1], other)
    pair.start()

    arrive(*outward(2))
    unpack(in_blocks.at[2], rows_fwd)
    gate_fwd = gates(rows_fwd)
    for at, weights in enumerate((near, far)):
        pre_gate = dot(rows_fwd[...], weights[0], 1, 1)
        pre_up = dot(rows_fwd[...], weights[1], 1, 1)
        fwd_hidden[...] = (pre_gate * jax.nn.sigmoid(pre_gate) * pre_up).astype(BF16)

        @slabs()
        def _(cols):
            part = gate_fwd * dot(fwd_hidden[...], weights[2, :, cols])
            grad_rows[:, cols] = grad_rows[:, cols] + part if at else part

    repack(grad_rows, back_out.at[1])
    issue(*homeward(1))

    pair.wait()
    vec_sum[...] = (vec[...] + vec_other[...]).astype(BF16)
    vecs[me] = vec_sum[...]

    def share_vec(act):
        @pl.loop(1, EXPERTS)
        def _(step):
            act(
                remote(
                    vec_sum,
                    vecs.at[me],
                    vec_send.at[step],
                    vec_recv.at[step],
                    {"expert": peer_of(me, step)},
                )
            )

    share_vec(lambda copy: copy.start())

    near_factors = ((mine.grad_gate, rows), (mine.grad_up, rows), (mine.hidden, scaled))
    for at, (left, right) in enumerate(near_factors):
        weight_grad(left.at[:, cuts[1]], right, near_last.at[at], None)

    arrive(*homeward(0))
    dnormed = combine(places_bwd, back_in.at[0])
    x_bwd, inverse, _ = norm_rows(saved_in[...], gain_row)
    scaled_grad = dnormed * gain_row
    mean = jnp.mean(scaled_grad * x_bwd, axis=-1, keepdims=True)
    in_grad = out_grad[...].astype(F32) + inverse * scaled_grad - x_bwd * inverse**3 * mean
    shift_out[0] = in_grad.astype(BF16)
    shift_bwd = remote(shift_out.at[0], sent_bwd, shift_send.at[0], shift_recv.at[0], ahead)
    shift_bwd.start()

    for at, (left, right) in enumerate(near_factors):
        there = there_grads.at[at, cuts[0]]
        grad_moves[0][at].wait()
        weight_grad(left.at[:, cuts[0]], right, there, there)
        total_moves[0][at].start()

    arrive(*homeward(1))
    mixed = fwd_in[...].astype(F32) + combine(places_fwd, back_in.at[1])
    shift_out[1] = mixed.astype(BF16)
    shift_fwd = remote(shift_out.at[1], sent_fwd, shift_send.at[1], shift_recv.at[1], after)
    shift_fwd.start()

    share_vec(lambda copy: copy.wait())
    gain_total[...] = jnp.sum(vecs[:, 16:32, :].astype(F32), axis=0)
    for at in range(16):
        router_total[:, at * 128 : (at + 1) * 128] = vecs[:, at, :].astype(F32)
    for at in range(3):
        there = there_grads.at[at, cuts[1]]
        grad_moves[1][at].wait()
        there[...] = (near_last[at] + there[...].astype(F32)).astype(BF16)
        total_moves[1][at].start()
    shift_bwd.wait()
    shift_fwd.wait()
    for moves in total_moves:
        for move in moves:
            move.wait()


def relay(*operands):
    fwd_in, router, w_down = operands[0], operands[4], operands[7]
    tokens, width = fwd_in.shape
    half = w_down.shape[0]
    packed = (EXPERTS * BLOCK, GROUPS * SLAB)
    pairs = EXPERTS * CAP
    vmem = pl.BlockSpec(memory_space=pltpu.VMEM)
    dma = pltpu.SemaphoreType.DMA
    hbm = pl.BlockSpec(memory_space=pl.ANY)
    out_shape = [
        jax.ShapeDtypeStruct((tokens, width), BF16),
        jax.ShapeDtypeStruct((tokens, width), BF16),
        jax.ShapeDtypeStruct((half, width), BF16),
        jax.ShapeDtypeStruct((half, width), BF16),
        jax.ShapeDtypeStruct((half, width), BF16),
        jax.ShapeDtypeStruct((EXPERTS, width), F32),
        jax.ShapeDtypeStruct((16, 128), F32),
    ]

    def kept(units):
        shape = (pairs, units)
        return [pltpu.VMEM(shape, F32)] * 2 + [pltpu.VMEM(shape, BF16)] * 3

    scratch = [
        pltpu.VMEM((GROUPS, packed[0], QUARTS * tokens), BF16),
        pltpu.VMEM((GROUPS, packed[0], QUARTS * tokens), BF16),
        pltpu.VMEM((3,) + packed, BF16),
        pltpu.VMEM((3,) + packed, BF16),
        pltpu.VMEM((pairs, width), BF16),
        pltpu.VMEM((pairs, width), BF16),
        pltpu.VMEM((pairs, width), BF16),
        pltpu.VMEM((3, half, width), BF16),
        pltpu.VMEM((3, half, width), BF16),
        *kept(half),
        *kept(FIRST),
        *kept(half - FIRST),
        pltpu.VMEM((pairs, half), BF16),
        pltpu.VMEM((pairs, width), F32),
        pltpu.VMEM((3, half, width), BF16),
        pltpu.VMEM((3, half, width), BF16),
        pltpu.VMEM((2,) + packed, BF16),
        pltpu.VMEM((2,) + packed, BF16),
        pltpu.VMEM((2, tokens, width), BF16),
        pltpu.VMEM((3, half - FIRST, width), F32),
        pltpu.VMEM((32, 128), F32),
        pltpu.VMEM((32, 128), F32),
        pltpu.VMEM((32, 128), BF16),
        pltpu.VMEM((EXPERTS, 32, 128), BF16),
        dma((3, EXPERTS)),
        dma((3, EXPERTS)),
        dma((2, EXPERTS)),
        dma((2, EXPERTS)),
        dma((5,)),
        dma((3,)),
        dma((2, 3)),
        dma((2, 3)),
        dma((2, 3)),
        dma((2, 3)),
        dma((2, 3)),
        dma((2,)),
        dma((2,)),
        dma((2,)),
        dma((EXPERTS,)),
        dma((EXPERTS,)),
    ]
    return pl.pallas_call(
        relay_kernel,
        out_shape=out_shape,
        in_specs=[vmem] * 5 + [hbm] * 3 + [vmem] * 2,
        out_specs=[hbm] * 5 + [vmem] * 2,
        scratch_shapes=scratch,
        compiler_params=pltpu.CompilerParams(
            collective_id=0, has_side_effects=True, vmem_limit_bytes=63 << 20
        ),
        name="relay",
    )(*operands)


def settle_kernel(*refs):
    count = (len(refs) - 2) // 3
    into, out_of = refs[-2], refs[-1]
    loads = [
        pltpu.make_async_copy(refs[at], refs[2 * count + at], into.at[at]) for at in range(count)
    ]
    stores = [
        pltpu.make_async_copy(refs[2 * count + at], refs[count + at], out_of.at[at])
        for at in range(count)
    ]
    for load in loads:
        load.start()
    for load, store in zip(loads, stores, strict=True):
        load.wait()
        store.start()
    for store in stores:
        store.wait()


def settle(arrays):
    hbm = pl.BlockSpec(memory_space=pl.ANY)
    sems = pltpu.SemaphoreType.DMA((len(arrays),))
    return pl.pallas_call(
        settle_kernel,
        out_shape=[jax.ShapeDtypeStruct(a.shape, a.dtype) for a in arrays],
        in_specs=[hbm] * len(arrays),
        out_specs=[hbm] * len(arrays),
        scratch_shapes=[pltpu.VMEM(a.shape, a.dtype) for a in arrays] + [sems, sems],
        compiler_params=pltpu.CompilerParams(vmem_limit_bytes=63 << 20),
        name="settle",
    )(*arrays)


def shards(fwd_in, saved_in, out_grad, gain, router, w_gate, w_up, w_down, routes_fwd, routes_bwd):
    results = relay(
        fwd_in[0],
        saved_in[0],
        out_grad[0],
        gain,
        router[0].T,
        w_gate[0, 0].T,
        w_up[0, 0].T,
        w_down[0, 0],
        routes_fwd[0].T,
        routes_bwd[0].T,
    )
    sent_fwd, sent_bwd, total_gate, total_up, total_down, router_total, gain_total = settle(results)
    return (
        sent_fwd[None],
        sent_bwd[None],
        total_gate.T[None, None],
        total_up.T[None, None],
        total_down[None, None],
        router_total.T[None],
        gain_total.reshape(1, -1),
    )


def solution(mesh):
    tokens = P("section", ("expert", "dp"), None)
    wide = P("section", "expert", None, "dp")
    deep = P("section", "expert", "dp", None)
    gain, router = P("section", None), P("section", None, None)
    return jax.shard_map(
        shards,
        mesh=mesh,
        in_specs=(tokens, tokens, tokens, gain, router, wide, wide, deep, tokens, tokens),
        out_specs=(tokens, tokens, wide, wide, deep, router, gain),
        check_vma=False,
    )
```

```python
import jax
import jax.numpy as jnp
from jax import lax
from jax.experimental import pallas as pl
from jax.experimental.pallas import tpu as pltpu
from jax.sharding import PartitionSpec as P

EPS = 1e-06
MESH = pl.DeviceIdType.MESH
EXPERTS = 32
CAP = 12
GROUPS = 3
QUARTS = 4
SLAB = 512
BLOCK = 16
FIRST = 256
F32 = jnp.float32
BF16 = jnp.bfloat16


def peer_of(me, step):
    return lax.rem(me // 4 + step // 4, 8) * 4 + lax.rem(me + step, 4)


def remote(src, dst, send_sem, recv_sem, device):
    return pltpu.make_async_remote_copy(
        src_ref=src,
        dst_ref=dst,
        send_sem=send_sem,
        recv_sem=recv_sem,
        device_id=device,
        device_id_type=MESH,
    )


def dot(left, right, left_dim=1, right_dim=0):
    return lax.dot_general(
        left, right, (((left_dim,), (right_dim,)), ((), ())), preferred_element_type=F32
    )


def norm_rows(inputs, gain_row):
    as_float = inputs.astype(F32)
    inverse = lax.rsqrt(jnp.mean(as_float * as_float, axis=-1, keepdims=True) + EPS)
    normed = (as_float * inverse * gain_row).astype(BF16)
    return as_float, inverse, normed


def place(places, routes):
    tokens = routes.shape[1]
    experts = lax.broadcasted_iota(jnp.int32, (EXPERTS, tokens), 0)
    named = (routes[0:1, :] == experts) | (routes[1:2, :] == experts)
    earlier = (
        lax.broadcasted_iota(jnp.int32, (tokens, tokens), 0)
        < lax.broadcasted_iota(jnp.int32, (tokens, tokens), 1)
    ).astype(F32)
    before = dot(named.astype(F32).astype(BF16), earlier.astype(BF16))
    slots = jnp.where(named, before, -1.0).astype(BF16)
    rows = EXPERTS * BLOCK
    row = lax.broadcasted_iota(jnp.int32, (rows, EXPERTS), 0)
    repeat = (row >> 4) == lax.broadcasted_iota(jnp.int32, (rows, EXPERTS), 1)
    wide = dot(repeat.astype(F32).astype(BF16), slots)
    row = lax.broadcasted_iota(jnp.int32, (rows, tokens), 0)
    quarter = (row >> 2) & 3
    slot = (row & 3).astype(F32)
    for group in range(GROUPS):
        hit = jnp.where(wide == slot + 4.0 * group, 1.0, 0.0)
        for q in range(QUARTS):
            places[group, :, q * tokens : (q + 1) * tokens] = jnp.where(
                quarter == q, hit, 0.0
            ).astype(BF16)


def pack(places, rows, packed):
    stacked = jnp.concatenate(
        [rows[:, q * SLAB : (q + 1) * SLAB] for q in range(QUARTS)], axis=0
    )
    for group in range(GROUPS):
        packed[:, group * SLAB : (group + 1) * SLAB] = dot(places[group], stacked).astype(BF16)


def combine(places, returned):
    total = dot(places[0], returned[:, 0:SLAB], 0, 0)
    for group in range(1, GROUPS):
        total = total + dot(places[group], returned[:, group * SLAB : (group + 1) * SLAB], 0, 0)
    tokens = total.shape[0] // QUARTS
    return jnp.concatenate(
        [total[q * tokens : (q + 1) * tokens] for q in range(QUARTS)], axis=1
    )


def shuffle():
    row = lax.broadcasted_iota(jnp.int32, (128, 128), 0)
    col = lax.broadcasted_iota(jnp.int32, (128, 128), 1)
    wanted = (((row >> 2) & 7) << 4) + ((row >> 5) << 2) + (row & 3)
    return jnp.where(col == wanted, 1.0, 0.0).astype(BF16)


def unpack(received, rows):
    order = shuffle()
    for at in range(4):
        part = dot(order, received[at * 128 : (at + 1) * 128, :]).astype(BF16)
        for group in range(GROUPS):
            for q in range(QUARTS):
                rows[
                    group * 128 + at * 32 : group * 128 + (at + 1) * 32,
                    q * SLAB : (q + 1) * SLAB,
                ] = part[q * 32 : (q + 1) * 32, group * SLAB : (group + 1) * SLAB]


def repack(rows, packed):
    order = shuffle()
    for at in range(4):
        for group in range(GROUPS):
            part = jnp.concatenate(
                [
                    rows[
                        group * 128 + at * 32 : group * 128 + (at + 1) * 32,
                        q * SLAB : (q + 1) * SLAB,
                    ]
                    for q in range(QUARTS)
                ],
                axis=0,
            ).astype(BF16)
            packed[at * 128 : (at + 1) * 128, group * SLAB : (group + 1) * SLAB] = dot(
                order, part, 0, 0
            ).astype(BF16)


def slabs():
    def over(body):
        @pl.loop(0, QUARTS)
        def _(q):
            body(pl.ds(pl.multiple_of(q * SLAB, SLAB), SLAB))

    return over


def pre_activate(rows, piece):
    piece.pre_gate[...] = dot(rows[...], piece.gate[...], 1, 1)
    piece.pre_up[...] = dot(rows[...], piece.up[...], 1, 1)


def backward_piece(scaled, piece):
    grad_hidden = dot(scaled[...], piece.down[...], 1, 1)
    pre_gate, pre_up = piece.pre_gate[...], piece.pre_up[...]
    sigm = jax.nn.sigmoid(pre_gate)
    swish = pre_gate * sigm
    hidden = (swish * pre_up).astype(BF16)
    piece.hidden[...] = hidden
    piece.grad_up[...] = (grad_hidden * swish).astype(BF16)
    piece.grad_gate[...] = (
        grad_hidden * pre_up * sigm * (1.0 + pre_gate * (1.0 - sigm))
    ).astype(BF16)
    return jnp.sum(hidden.astype(F32) * grad_hidden, axis=1, keepdims=True)


def row_grads(piece, grad_rows, add):
    @slabs()
    def _(cols):
        part = dot(piece.grad_gate[...], piece.gate[:, cols])
        part = part + dot(piece.grad_up[...], piece.up[:, cols])
        grad_rows[:, cols] = grad_rows[:, cols] + part if add else part


def weight_grad(left, right, left_there, right_there, target):
    turned, turned_there = left[...].T, left_there[...].T

    @slabs()
    def _(cols):
        part = dot(turned, right[:, cols]) + dot(turned_there, right_there[:, cols])
        target[:, cols] = part.astype(BF16)


class Piece:
    def __init__(self, weights, kept):
        self.gate, self.up, self.down = weights
        self.pre_gate, self.pre_up, self.hidden, self.grad_gate, self.grad_up = kept


def relay_kernel(*refs):
    refs = list(refs)

    def take(count):
        taken = refs[:count]
        del refs[:count]
        return taken

    fwd_in, saved_in, out_grad, gain, router = take(5)
    own_hbm = take(3)
    routes_fwd, routes_bwd = take(2)
    sent_fwd, sent_bwd = take(2)
    totals = take(3)
    router_total, gain_total = take(2)
    places_fwd, places_bwd, out_blocks, in_blocks, rows, scaled, rows_fwd, near, far = take(9)
    kept_near, kept_first, kept_last = take(5), take(5), take(5)
    there_first, there_last = take(3), take(3)
    there_rows, fwd_hidden, grad_rows, sums, back_out, back_in, shift_out = take(7)
    vec, vec_other, vec_sum, vecs = take(4)
    out_send, out_recv, back_send, back_recv, local = take(5)
    near_sems, far_send, far_recv, grad_send, grad_recv, total_sems = take(6)
    row_send, row_recv = take(2)
    shift_send, shift_recv, pair_sems, vec_send, vec_recv = take(5)

    me = lax.axis_index("expert")
    other = {"dp": 1 - lax.axis_index("dp")}
    section = lax.axis_index("section")
    after = {"section": lax.rem(section + 1, 4)}
    ahead = {"section": lax.rem(section + 3, 4)}
    half = near.shape[1]
    cuts = (slice(0, FIRST), slice(FIRST, half))

    barrier = pltpu.get_barrier_semaphore()

    @pl.loop(1, EXPERTS)
    def _(step):
        pl.semaphore_signal(
            barrier, inc=1, device_id={"expert": peer_of(me, step)}, device_id_type=MESH
        )

    for device in (other, after, ahead):
        pl.semaphore_signal(barrier, inc=1, device_id=device, device_id_type=MESH)

    near_moves = [
        pltpu.make_async_copy(own_hbm[at], near.at[at], near_sems.at[at]) for at in range(3)
    ]
    for move in near_moves:
        move.start()

    def block(of):
        return pl.ds(pl.multiple_of(of * BLOCK, BLOCK), BLOCK)

    def each(sources, targets, send, recv, act):
        @pl.loop(1, EXPERTS)
        def _(step):
            peer = peer_of(me, step)
            act(
                remote(
                    sources.at[block(peer)],
                    targets.at[block(me)],
                    send.at[step],
                    recv.at[step],
                    {"expert": peer},
                )
            )

    def own_block(sources, targets, sem):
        return pltpu.make_async_copy(sources.at[block(me)], targets.at[block(me)], sem)

    def issue(sources, targets, send, recv, sem):
        each(sources, targets, send, recv, lambda copy: copy.start())
        own_block(sources, targets, sem).start()

    def arrive(sources, targets, send, recv, sem):
        own_block(sources, targets, sem).wait()
        each(sources, targets, send, recv, lambda copy: copy.wait())

    def outward(at):
        return (
            out_blocks.at[at], in_blocks.at[at], out_send.at[at], out_recv.at[at], local.at[at],
        )

    def homeward(at):
        return (
            back_out.at[at], back_in.at[at], back_send.at[at], back_recv.at[at], local.at[3 + at],
        )

    weight_moves = [
        [
            remote(
                own_hbm[at].at[cut],
                far.at[at, cut],
                far_send.at[turn, at],
                far_recv.at[turn, at],
                other,
            )
            for at in range(3)
        ]
        for turn, cut in enumerate(cuts)
    ]
    row_moves = [
        remote(mine_rows, there_rows.at[at], row_send.at[at], row_recv.at[at], other)
        for at, mine_rows in enumerate((rows, scaled))
    ]
    grad_moves = [
        [
            remote(kept[2 + at], there[at], grad_send.at[turn, at], grad_recv.at[turn, at], other)
            for at in range(3)
        ]
        for turn, (kept, there) in enumerate(
            ((kept_first, there_first), (kept_last, there_last))
        )
    ]
    total_moves = [
        [
            pltpu.make_async_copy(
                sums.at[at, cut], totals[(at + 2) % 3].at[cut], total_sems.at[turn, at]
            )
            for at in range(3)
        ]
        for turn, cut in enumerate(cuts)
    ]
    mine = Piece([near.at[at] for at in range(3)], kept_near)
    first = Piece([far.at[at, cuts[0]] for at in range(3)], kept_first)
    last = Piece([far.at[at, cuts[1]] for at in range(3)], kept_last)

    gain_row = gain[...].astype(F32)
    place(places_bwd, routes_bwd)
    normed = norm_rows(saved_in[...], gain_row)[2]
    pack(places_bwd, normed, out_blocks.at[0])

    pl.semaphore_wait(barrier, EXPERTS + 2)
    for move in weight_moves[0]:
        move.start()
    issue(*outward(0))
    for move in weight_moves[1]:
        move.start()
    pack(places_bwd, out_grad[...], out_blocks.at[1])
    issue(*outward(1))
    place(places_fwd, routes_fwd)
    normed = norm_rows(fwd_in[...], gain_row)[2]
    pack(places_fwd, normed, out_blocks.at[2])

    lanes = lax.broadcasted_iota(jnp.int32, (rows.shape[0], EXPERTS), 1)

    def gates(of):
        logits = dot(of[...], router[...], 1, 1)
        return jax.nn.sigmoid(jnp.sum(jnp.where(lanes == me, logits, 0.0), axis=1, keepdims=True))

    def send_grads(turn):
        for move in grad_moves[turn]:
            move.start()

    arrive(*outward(0))
    issue(*outward(2))
    unpack(in_blocks.at[0], rows)
    row_moves[0].start()
    gate_bwd = gates(rows)
    for move in near_moves:
        move.wait()
    pre_activate(rows, mine)
    for move in weight_moves[0]:
        move.wait()
    pre_activate(rows, first)

    arrive(*outward(1))
    unpack(in_blocks.at[1], scaled)

    @slabs()
    def _(cols):
        scaled[:, cols] = (gate_bwd * scaled[:, cols].astype(F32)).astype(BF16)

    row_moves[1].start()
    share = backward_piece(scaled, first)
    send_grads(0)
    share = share + backward_piece(scaled, mine)
    row_grads(first, grad_rows, False)
    row_grads(mine, grad_rows, True)
    for move in weight_moves[1]:
        move.wait()
    pre_activate(rows, last)
    share = share + backward_piece(scaled, last)
    send_grads(1)
    row_grads(last, grad_rows, True)

    dlogit = (share * (1.0 - gate_bwd)).astype(BF16).astype(F32)
    row = lax.broadcasted_iota(jnp.int32, router.shape, 0)

    @slabs()
    def _(cols):
        part = dlogit * jnp.sum(
            jnp.where(row[:, 0:SLAB] == me, router[:, cols].astype(F32), 0.0),
            axis=0,
            keepdims=True,
        )
        grad_rows[:, cols] = grad_rows[:, cols] + part

    repack(grad_rows, back_out.at[0])
    issue(*homeward(0))
    for q in range(QUARTS):
        cols = slice(q * SLAB, (q + 1) * SLAB)
        rows_float = rows[:, cols].astype(F32)
        router_column = jnp.sum(rows_float * dlogit, axis=0, keepdims=True)
        gain_part = jnp.sum(rows_float * grad_rows[:, cols], axis=0, keepdims=True)
        gain_part = gain_part / gain_row[:, cols]
        for at in range(4):
            vec[q * 4 + at : q * 4 + at + 1, :] = router_column[:, at * 128 : (at + 1) * 128]
            vec[16 + q * 4 + at : 17 + q * 4 + at, :] = gain_part[:, at * 128 : (at + 1) * 128]
    pair = remote(vec, vec_other, pair_sems.at[0], pair_sems.at[1], other)
    pair.start()

    arrive(*outward(2))
    unpack(in_blocks.at[2], rows_fwd)
    gate_fwd = gates(rows_fwd)
    for at, weights in enumerate((near, far)):
        pre_gate = dot(rows_fwd[...], weights[0], 1, 1)
        pre_up = dot(rows_fwd[...], weights[1], 1, 1)
        fwd_hidden[...] = (pre_gate * jax.nn.sigmoid(pre_gate) * pre_up).astype(BF16)

        @slabs()
        def _(cols):
            part = gate_fwd * dot(fwd_hidden[...], weights[2, :, cols])
            grad_rows[:, cols] = grad_rows[:, cols] + part if at else part

    repack(grad_rows, back_out.at[1])
    issue(*homeward(1))

    pair.wait()
    vec_sum[...] = (vec[...] + vec_other[...]).astype(BF16)
    vecs[me] = vec_sum[...]

    def share_vec(act):
        @pl.loop(1, EXPERTS)
        def _(step):
            act(
                remote(
                    vec_sum,
                    vecs.at[me],
                    vec_send.at[step],
                    vec_recv.at[step],
                    {"expert": peer_of(me, step)},
                )
            )

    share_vec(lambda copy: copy.start())

    arrive(*homeward(0))
    dnormed = combine(places_bwd, back_in.at[0])
    x_bwd, inverse, _ = norm_rows(saved_in[...], gain_row)
    scaled_grad = dnormed * gain_row
    mean = jnp.mean(scaled_grad * x_bwd, axis=-1, keepdims=True)
    in_grad = out_grad[...].astype(F32) + inverse * scaled_grad - x_bwd * inverse**3 * mean
    shift_out[0] = in_grad.astype(BF16)
    shift_bwd = remote(shift_out.at[0], sent_bwd, shift_send.at[0], shift_recv.at[0], ahead)
    shift_bwd.start()

    rights = ((scaled, there_rows.at[1]), (rows, there_rows.at[0]), (rows, there_rows.at[0]))
    lefts = (mine.hidden, mine.grad_gate, mine.grad_up)
    for move in row_moves:
        move.wait()

    def finish(turn):
        cut = cuts[turn]
        there = (there_first, there_last)[turn]
        for at in range(3):
            grad_moves[turn][at].wait()
            weight_grad(
                lefts[at].at[:, cut],
                rights[at][0],
                there[at],
                rights[at][1],
                sums.at[at, cut],
            )
            total_moves[turn][at].start()

    finish(0)
    arrive(*homeward(1))
    mixed = fwd_in[...].astype(F32) + combine(places_fwd, back_in.at[1])
    shift_out[1] = mixed.astype(BF16)
    shift_fwd = remote(shift_out.at[1], sent_fwd, shift_send.at[1], shift_recv.at[1], after)
    shift_fwd.start()

    share_vec(lambda copy: copy.wait())
    gain_total[...] = jnp.sum(vecs[:, 16:32, :].astype(F32), axis=0)
    for at in range(16):
        router_total[:, at * 128 : (at + 1) * 128] = vecs[:, at, :].astype(F32)
    finish(1)
    shift_bwd.wait()
    shift_fwd.wait()
    for moves in total_moves:
        for move in moves:
            move.wait()


def relay(*operands):
    fwd_in, router, w_down = operands[0], operands[4], operands[7]
    tokens, width = fwd_in.shape
    half = w_down.shape[0]
    packed = (EXPERTS * BLOCK, GROUPS * SLAB)
    pairs = EXPERTS * CAP
    vmem = pl.BlockSpec(memory_space=pltpu.VMEM)
    dma = pltpu.SemaphoreType.DMA
    hbm = pl.BlockSpec(memory_space=pl.ANY)
    out_shape = [
        jax.ShapeDtypeStruct((tokens, width), BF16),
        jax.ShapeDtypeStruct((tokens, width), BF16),
        jax.ShapeDtypeStruct((half, width), BF16),
        jax.ShapeDtypeStruct((half, width), BF16),
        jax.ShapeDtypeStruct((half, width), BF16),
        jax.ShapeDtypeStruct((EXPERTS, width), F32),
        jax.ShapeDtypeStruct((16, 128), F32),
    ]

    def kept(units):
        shape = (pairs, units)
        return [pltpu.VMEM(shape, F32)] * 2 + [pltpu.VMEM(shape, BF16)] * 3

    scratch = [
        pltpu.VMEM((GROUPS, packed[0], QUARTS * tokens), BF16),
        pltpu.VMEM((GROUPS, packed[0], QUARTS * tokens), BF16),
        pltpu.VMEM((3,) + packed, BF16),
        pltpu.VMEM((3,) + packed, BF16),
        pltpu.VMEM((pairs, width), BF16),
        pltpu.VMEM((pairs, width), BF16),
        pltpu.VMEM((pairs, width), BF16),
        pltpu.VMEM((3, half, width), BF16),
        pltpu.VMEM((3, half, width), BF16),
        *kept(half),
        *kept(FIRST),
        *kept(half - FIRST),
        *kept(FIRST)[2:],
        *kept(half - FIRST)[2:],
        pltpu.VMEM((2, pairs, width), BF16),
        pltpu.VMEM((pairs, half), BF16),
        pltpu.VMEM((pairs, width), F32),
        pltpu.VMEM((3, half, width), BF16),
        pltpu.VMEM((2,) + packed, BF16),
        pltpu.VMEM((2,) + packed, BF16),
        pltpu.VMEM((2, tokens, width), BF16),
        pltpu.VMEM((32, 128), F32),
        pltpu.VMEM((32, 128), F32),
        pltpu.VMEM((32, 128), BF16),
        pltpu.VMEM((EXPERTS, 32, 128), BF16),
        dma((3, EXPERTS)),
        dma((3, EXPERTS)),
        dma((2, EXPERTS)),
        dma((2, EXPERTS)),
        dma((5,)),
        dma((3,)),
        dma((2, 3)),
        dma((2, 3)),
        dma((2, 3)),
        dma((2, 3)),
        dma((2, 3)),
        dma((2,)),
        dma((2,)),
        dma((2,)),
        dma((2,)),
        dma((2,)),
        dma((EXPERTS,)),
        dma((EXPERTS,)),
    ]
    return pl.pallas_call(
        relay_kernel,
        out_shape=out_shape,
        in_specs=[vmem] * 5 + [hbm] * 3 + [vmem] * 2,
        out_specs=[hbm] * 5 + [vmem] * 2,
        scratch_shapes=scratch,
        compiler_params=pltpu.CompilerParams(
            collective_id=0, has_side_effects=True, vmem_limit_bytes=63 << 20
        ),
        name="relay",
    )(*operands)


def settle_kernel(*refs):
    count = (len(refs) - 2) // 3
    into, out_of = refs[-2], refs[-1]
    loads = [
        pltpu.make_async_copy(refs[at], refs[2 * count + at], into.at[at]) for at in range(count)
    ]
    stores = [
        pltpu.make_async_copy(refs[2 * count + at], refs[count + at], out_of.at[at])
        for at in range(count)
    ]
    for load in loads:
        load.start()
    for load, store in zip(loads, stores, strict=True):
        load.wait()
        store.start()
    for store in stores:
        store.wait()


def settle(arrays):
    hbm = pl.BlockSpec(memory_space=pl.ANY)
    sems = pltpu.SemaphoreType.DMA((len(arrays),))
    return pl.pallas_call(
        settle_kernel,
        out_shape=[jax.ShapeDtypeStruct(a.shape, a.dtype) for a in arrays],
        in_specs=[hbm] * len(arrays),
        out_specs=[hbm] * len(arrays),
        scratch_shapes=[pltpu.VMEM(a.shape, a.dtype) for a in arrays] + [sems, sems],
        compiler_params=pltpu.CompilerParams(vmem_limit_bytes=63 << 20),
        name="settle",
    )(*arrays)


def shards(fwd_in, saved_in, out_grad, gain, router, w_gate, w_up, w_down, routes_fwd, routes_bwd):
    results = relay(
        fwd_in[0],
        saved_in[0],
        out_grad[0],
        gain,
        router[0].T,
        w_gate[0, 0].T,
        w_up[0, 0].T,
        w_down[0, 0],
        routes_fwd[0].T,
        routes_bwd[0].T,
    )
    sent_fwd, sent_bwd, total_gate, total_up, total_down, router_total, gain_total = settle(results)
    return (
        sent_fwd[None],
        sent_bwd[None],
        total_gate.T[None, None],
        total_up.T[None, None],
        total_down[None, None],
        router_total.T[None],
        gain_total.reshape(1, -1),
    )


def solution(mesh):
    tokens = P("section", ("expert", "dp"), None)
    wide = P("section", "expert", None, "dp")
    deep = P("section", "expert", "dp", None)
    gain, router = P("section", None), P("section", None, None)
    return jax.shard_map(
        shards,
        mesh=mesh,
        in_specs=(tokens, tokens, tokens, gain, router, wide, wide, deep, tokens, tokens),
        out_specs=(tokens, tokens, wide, wide, deep, router, gain),
        check_vma=False,
    )
```
